32 devices in a mesh: groups: 2 (over x), hist: 16 (over z, y, core).
Axes of the slice: x: 2, y: 2, z: 4, core: 2. Of those that a mesh axis runs over, the one named last changes fastest.
Arguments:
- queries: bfloat16 [256, 1536], P(('groups', 'hist')), parts along dimension 0, may hold values from -6 to 6
- keys_cache: bfloat16 [32768, 1536], P(('groups', 'hist')), parts along dimension 0, may hold values from -6 to 6
- values_cache: bfloat16 [32768, 1536], P(('groups', 'hist')), parts along dimension 0, may hold values from -6 to 6
- sel_blocks: int32 [64], P('groups'), parts along dimension 0, may hold values from 0 to 127, as said below
- hist_len: int32 [2], P('groups'), parts along dimension 0, may hold values from 8192 to 16384
- w_gate: bfloat16 [1536, 6144], P(None, 'hist'), may hold values from -0.15625 to 0.15625
- w_up: bfloat16 [1536, 6144], P(None, 'hist'), may hold values from -0.15625 to 0.15625
- w_down: bfloat16 [6144, 1536], P('hist'), may hold values from -0.078125 to 0.078125
Outputs:
- scored: bfloat16 [256, 1536], P(('groups', 'hist')), parts along dimension 0
The draws below stay inside these ranges and needn't reach their ends.
There are 2 independent parts, one for each index of `groups`. The reference program is written for one: setup_inputs(seed, part) draws one part's arguments, and reference() takes and returns one part's arrays. A program takes and returns all parts, laid end to end along the dimension named above; an argument that names none is the same for every part. Nothing has to cross between parts.
Inputs may be any that keep to these rules, and one draw needn't show every extreme that they name: `sel_blocks`: ascending and distinct block numbers; block b holds keys b * 128 to (b + 1) * 128 - 1; of every aligned run of 8 blocks at most 4 are selected, and some run has exactly 4.
All inputs are finite; a program needn't handle non-finite values.
Results may differ from the reference program's by a relative error of at most 0.0051.
Values may be sent and summed in bfloat16 or wider, within the bound.
A program may use at most 128 MiB of HBM per device.

```python
import math
import jax
import jax.numpy as jnp
from jax import lax

HDIM = 128
D = 1536
FF = 6144
BLOCK = 128
BLK_DEV = 8
QT = 128
HIST = 16384
SELB = 32


def draw_sel_blocks(key, part):
    devices = SELB // 2
    key_perm, key_rank = jax.random.split(jax.random.fold_in(key, 11))
    quarter = devices // 4
    device_ids = jnp.arange(devices, dtype=jnp.int32)
    pattern = jnp.where(device_ids < quarter, 4, jnp.where(device_ids < 2 * quarter, 0, 2)).astype(jnp.int32)
    counts = jax.random.permutation(key_perm, pattern)
    tickets = jax.random.randint(key_rank, (devices, BLK_DEV), 0, 1 << 20) * BLK_DEV + jnp.arange(BLK_DEV, dtype=jnp.int32)[None, :]
    ordering = jnp.argsort(tickets, axis=1)
    ranking = jnp.argsort(ordering, axis=1)
    chosen = (ranking < counts[:, None]).reshape(-1)
    block_ids = jnp.arange(devices * BLK_DEV, dtype=jnp.int32)
    sort_keys = jnp.where(chosen, block_ids, devices * BLK_DEV + block_ids)
    return jnp.sort(sort_keys)[:SELB].astype(jnp.int32)


def steps_of(stream_key, dims, shards, smallest, top_value):
    def one(position, blocks):
        heights = jax.random.uniform(jax.random.fold_in(jax.random.fold_in(stream_key, 6), position), (blocks,), jnp.float32, smallest / len(shards), top_value / len(shards))
        return jnp.repeat(jnp.exp(heights), dims[position] // blocks).reshape((-1,) + (1,) * (len(dims) - position - 1))

    factor_of = one(*shards[0])
    for cut in shards[1:]:
        factor_of = factor_of * one(*cut)
    return factor_of


def centred(own_key, shape, width, most, cuts=(), kind=jnp.bfloat16):
    array = width * jax.random.normal(own_key, shape, jnp.float32)
    if cuts:
        array = array * steps_of(own_key, shape, cuts, -0.22, 0.18)
    return jnp.clip(array, -most, most).astype(kind)


def setup_inputs(seed: int = 0, part: int = 0) -> dict:
    keys = jax.random.split(jax.random.key(seed), 9)
    part_splits = jax.random.split(jax.random.fold_in(keys[8], part), 9)
    return {
        "queries": centred(part_splits[0], (QT, D), 1.0, 6.0, ((0, 16),)),
        "keys_cache": centred(part_splits[1], (HIST, D), 1.0, 6.0, ((0, 16),)),
        "values_cache": centred(part_splits[2], (HIST, D), 1.0, 6.0, ((0, 16),)),
        "sel_blocks": draw_sel_blocks(jax.random.fold_in(jax.random.fold_in(keys[8], part), 71), part),
        "hist_len": jax.random.randint(part_splits[4], (1,), HIST // 2, HIST + 1).astype(jnp.int32),
        "w_gate": centred(keys[5], (D, FF), D ** -0.5, 0.15625, ((1, 16),)),
        "w_up": centred(keys[6], (D, FF), D ** -0.5, 0.15625, ((1, 16),)),
        "w_down": centred(keys[7], (FF, D), FF ** -0.5, 0.078125, ((0, 16),)),
    }


def rms_norm(values):
    return values * lax.rsqrt(lax.optimization_barrier(jnp.mean(values * values, axis=-1, keepdims=True)) + 1e-06)

def reference(queries, keys_cache, values_cache, sel_blocks, hist_len, w_gate, w_up, w_down):
    model_width = queries.shape[1]
    head_count = model_width // HDIM
    key_index = (sel_blocks[:, None] * BLOCK + jnp.arange(BLOCK, dtype=jnp.int32)[None, :]).reshape(-1).astype(jnp.int32)
    live_weight = (key_index < hist_len[0]).astype(jnp.float32)
    key_heads = keys_cache[key_index].reshape(-1, head_count, HDIM).transpose(1, 0, 2)
    value_heads = values_cache[key_index].reshape(-1, head_count, HDIM).transpose(1, 0, 2)
    query_heads = queries.reshape(-1, head_count, HDIM).transpose(1, 0, 2)
    inv_scale = 1.0 / math.sqrt(HDIM)

    def one_head(operands):
        query_part, key_part, value_part = operands
        scores = jnp.dot(query_part, key_part.T, preferred_element_type=jnp.float32) * inv_scale
        weights = (jax.nn.silu(scores) * live_weight[None, :]).astype(jnp.bfloat16)
        return jnp.dot(weights, value_part, preferred_element_type=jnp.float32)
    per_head = lax.map(one_head, (query_heads, key_heads, value_heads))
    attention = per_head.transpose(1, 0, 2).reshape(-1, model_width)
    stream = queries.astype(jnp.float32) + rms_norm(attention)
    normed = rms_norm(stream).astype(jnp.bfloat16)
    gate_proj = jnp.dot(normed, w_gate, preferred_element_type=jnp.float32)
    up_proj = jnp.dot(normed, w_up, preferred_element_type=jnp.float32)
    activation = (jax.nn.silu(gate_proj) * up_proj).astype(jnp.bfloat16)
    ffn_out = jnp.dot(activation, w_down, preferred_element_type=jnp.float32)
    return (stream + ffn_out).astype(jnp.bfloat16)
```

```python
import functools
import math

import jax
import jax.numpy as jnp
from jax import lax
from jax.experimental import pallas as pl
from jax.experimental.pallas import tpu as pltpu
from jax.sharding import PartitionSpec as P

HDIM = 128
BLOCK = 128
CORES = 2
MESH = pl.DeviceIdType.MESH
F32 = jnp.float32
BF16 = jnp.bfloat16


def loop(start, stop, body):
    if stop - start <= 8:
        for i in range(start, stop):
            body(i)
    else:
        lax.fori_loop(start, stop, lambda i, c: (body(i), c)[1], 0)


def silu_of_twice(z):
    return z + z * jnp.tanh(z)


def pack(rows):
    half = rows.shape[1] // 2
    return jnp.concatenate([rows[:, :half], rows[:, half:]], axis=0)


def unpack(rows):
    half = rows.shape[0] // 2
    return jnp.concatenate([rows[:half], rows[half:]], axis=1)


def rms_scale(packed):
    half, width = packed.shape[0] // 2, packed.shape[1] * 2
    squares = jnp.sum(packed * packed, axis=1, keepdims=True)
    both = lax.rsqrt((squares[:half] + squares[half:]) / width + 1e-06)
    return jnp.concatenate([both, both], axis=0)


def kernel(
    chips, sel_ref, len_ref, q_ref, k_hbm, v_hbm, wg_hbm, wu_hbm, wd_hbm, out_ref,
    qbuf, nbuf, keep_a, stage_a, cbuf_a, obuf_a, rbuf_a, keep_f, stage_f, cbuf_f, obuf_f, rbuf_f,
    k_all, v_all, k_sel, v_sel, wg, wu, wd,
    local_sem, q_send, q_recv, qf_send, qf_recv, n_send, n_recv, nf_send, nf_recv,
    a_send, a_recv, f_send, f_recv, c_send, c_recv,
):
    tokens, width = q_ref.shape
    half = width // 2
    pairs = half // HDIM
    slots = k_sel.shape[0]
    blocks_dev = k_all.shape[0]
    chunk = min(chips, 8)
    group = lax.axis_index("groups")
    me = lax.axis_index("hist")
    chip, core = me // CORES, me % CORES
    sibling = (group, chip * CORES + (1 - core))

    def peer(offset):
        return (group, lax.rem(chip + offset, chips) * CORES + core)

    locals_ = [
        pltpu.make_async_copy(src, dst, local_sem.at[i])
        for i, (src, dst) in enumerate(
            [(k_hbm, k_all), (v_hbm, v_all), (wg_hbm, wg), (wu_hbm, wu), (wd_hbm, wd)]
        )
    ]
    for copy in locals_:
        copy.start()

    barrier = pltpu.get_barrier_semaphore()
    pl.semaphore_signal(barrier, inc=1, device_id=sibling, device_id_type=MESH)
    loop(1, chips, lambda k: pl.semaphore_signal(barrier, inc=1, device_id=peer(k), device_id_type=MESH))

    q_packed = pack(q_ref[...].astype(F32))
    qbuf[0, 0] = q_packed.astype(BF16)
    pl.semaphore_wait(barrier, chips)

    class Gather:
        def __init__(self, buf, send, recv, fsend, frecv):
            self.buf, self.sems = buf, (send, recv, fsend, frecv)

        def out(self, k):
            send, recv, _, _ = self.sems
            return pltpu.make_async_remote_copy(
                self.buf.at[0, 0], self.buf.at[0, k], send.at[k], recv.at[k], peer(k), MESH
            )

        def forward(self, k):
            _, _, fsend, frecv = self.sems
            return pltpu.make_async_remote_copy(
                self.buf.at[0, k], self.buf.at[1, k], fsend.at[k], frecv.at[k], sibling, MESH
            )

        def start(self):
            loop(1, chips, lambda k: self.out(k).start())
            self.forward(0).start()

        def finish(self):
            def step(k):
                self.out(k).wait_recv()
                self.forward(k).start()

            loop(1, chips, step)
            loop(0, chips, lambda k: self.forward(k).wait_recv())

        def drain(self):
            loop(1, chips, lambda k: self.out(k).wait_send())
            loop(0, chips, lambda k: self.forward(k).wait_send())

    class Scatter:
        def __init__(self, index, keep, stage, cbuf, obuf, rbuf, send, recv):
            self.keep, self.stage, self.cbuf, self.obuf, self.rbuf = keep, stage, cbuf, obuf, rbuf
            self.index, self.send, self.recv = index, send, recv

        def across(self):
            return pltpu.make_async_remote_copy(
                self.stage, self.cbuf, c_send.at[self.index], c_recv.at[self.index], sibling, MESH
            )

        def out(self, k):
            return pltpu.make_async_remote_copy(
                self.obuf.at[k], self.rbuf.at[k], self.send.at[k], self.recv.at[k], peer(chips - k), MESH
            )

        def total(self):
            self.across().start()
            self.across().wait_recv()

            def step(k):
                self.obuf[k] = (self.keep[k] + self.cbuf[k].astype(F32)).astype(BF16)
                self.out(k).start()

            loop(1, chips, step)
            total = self.keep[0] + self.cbuf[0].astype(F32)
            if chips <= 8:
                for k in range(1, chips):
                    self.out(k).wait_recv()
                    total = total + self.rbuf[k].astype(F32)
                return total

            def add(k, total):
                self.out(k).wait_recv()
                return total + self.rbuf[k].astype(F32)

            return lax.fori_loop(1, chips, add, total)

        def drain(self):
            self.across().wait_send()
            loop(1, chips, lambda k: self.out(k).wait_send())

    queries = Gather(qbuf, q_send, q_recv, qf_send, qf_recv)
    attended = Scatter(0, keep_a, stage_a, cbuf_a, obuf_a, rbuf_a, a_send, a_recv)
    normals = Gather(nbuf, n_send, n_recv, nf_send, nf_recv)
    hidden = Scatter(1, keep_f, stage_f, cbuf_f, obuf_f, rbuf_f, f_send, f_recv)

    queries.start()

    first = me * blocks_dev

    def pick(i, state):
        count, chosen, used = state
        local = sel_ref[i] - first
        mine = jnp.logical_and(local >= 0, local < blocks_dev)
        hit = [jnp.logical_and(mine, count == s) for s in range(slots)]
        chosen = tuple(jnp.where(h, local, c) for h, c in zip(hit, chosen))
        return count + mine.astype(jnp.int32), chosen, used

    zero = jnp.int32(0)
    count, chosen, _ = lax.fori_loop(0, sel_ref.shape[0], pick, (zero, (zero,) * slots, zero))
    row = lax.broadcasted_iota(jnp.int32, (BLOCK, 1), 0)
    locals_[0].wait()
    for s in range(slots):
        k_sel[s] = k_all[chosen[s]]
    locals_[1].wait()
    for s in range(slots):
        limit = jnp.where(count > s, len_ref[0] - (first + chosen[s]) * BLOCK, 0)
        block = v_all[chosen[s]]
        v_sel[s] = jnp.where(row < limit, block.astype(F32), 0.0).astype(BF16)

    queries.finish()

    half_scale = 0.5 / math.sqrt(HDIM)

    def head(query, columns):
        keys = k_sel[:, :, columns].reshape(slots * BLOCK, HDIM)
        values = v_sel[:, :, columns].reshape(slots * BLOCK, HDIM)
        scores = lax.dot_general(query, keys, (((1,), (1,)), ((), ())), preferred_element_type=F32)
        weights = silu_of_twice(scores * half_scale).astype(BF16)
        return jnp.dot(weights, values, preferred_element_type=F32)

    def halves(block):
        w = block.shape[-1]
        block = block.astype(F32).reshape(2 * chunk, 2, tokens, w)
        return [block[:, i].reshape(2 * chunk * tokens, w).astype(BF16) for i in range(2)]

    def joined(left, right):
        w = left.shape[-1]
        parts = [x.reshape(2, chunk, tokens, w) for x in (left, right)]
        return jnp.concatenate(parts, axis=2)

    def attend(i):
        rows = pl.ds(i * chunk, chunk)
        for j in range(pairs):
            columns = pl.ds(j * HDIM, HDIM)
            left, right = halves(qbuf[:, rows, :, columns])
            both = joined(head(left, columns), head(right, pl.ds(half + j * HDIM, HDIM)))
            keep_a[rows, :, columns] = both[0]
            stage_a[rows, :, columns] = both[1].astype(BF16)

    loop(0, chips // chunk, attend)

    attention = attended.total()
    stream = q_packed + attention * rms_scale(attention)
    nbuf[0, 0] = (stream * rms_scale(stream)).astype(BF16)
    normals.start()
    for copy in locals_[2:]:
        copy.wait()
    normals.finish()

    step_columns = 256 if half % 256 == 0 else HDIM

    def feed(i):
        rows = pl.ds(i * chunk, chunk)
        left, right = halves(nbuf[:, rows])

        def project(w):
            top = jnp.dot(left, w[:half], preferred_element_type=F32)
            return top + jnp.dot(right, w[half:], preferred_element_type=F32)

        activation = (silu_of_twice(0.5 * project(wg)) * project(wu)).astype(BF16)
        for j in range(half // step_columns):
            columns = pl.ds(j * step_columns, step_columns)
            both = joined(
                jnp.dot(activation, wd[:, columns], preferred_element_type=F32),
                jnp.dot(activation, wd[:, pl.ds(half + j * step_columns, step_columns)], preferred_element_type=F32),
            )
            keep_f[rows, :, columns] = both[0]
            stage_f[rows, :, columns] = both[1].astype(BF16)

    loop(0, chips // chunk, feed)

    out_ref[...] = unpack(stream + hidden.total()).astype(out_ref.dtype)

    queries.drain()
    attended.drain()
    normals.drain()
    hidden.drain()


def on_device(hist, queries, keys_cache, values_cache, sel_blocks, hist_len, w_gate, w_up, w_down):
    chips = hist // CORES
    tokens, width = queries.shape
    blocks_dev = keys_cache.shape[0] // BLOCK
    slots = max(1, blocks_dev // 2)
    hidden = w_gate.shape[1]
    blocked = (blocks_dev, BLOCK, width)
    packed = (2 * tokens, width // 2)
    exchange = [
        pltpu.VMEM((chips,) + packed, F32),
        pltpu.VMEM((chips,) + packed, BF16),
        pltpu.VMEM((chips,) + packed, BF16),
        pltpu.VMEM((chips,) + packed, BF16),
        pltpu.VMEM((chips,) + packed, BF16),
    ]
    smem = pl.BlockSpec(memory_space=pltpu.SMEM)
    vmem = pl.BlockSpec(memory_space=pltpu.VMEM)
    anywhere = pl.BlockSpec(memory_space=pl.ANY)
    return pl.pallas_call(
        functools.partial(kernel, chips),
        out_shape=jax.ShapeDtypeStruct((tokens, width), BF16),
        in_specs=[smem, smem, vmem] + [anywhere] * 5,
        out_specs=vmem,
        scratch_shapes=[
            pltpu.VMEM((2, chips) + packed, BF16),
            pltpu.VMEM((2, chips) + packed, BF16),
            *exchange,
            *exchange,
            pltpu.VMEM(blocked, BF16),
            pltpu.VMEM(blocked, BF16),
            pltpu.VMEM((slots, BLOCK, width), BF16),
            pltpu.VMEM((slots, BLOCK, width), BF16),
            pltpu.VMEM((width, hidden), BF16),
            pltpu.VMEM((width, hidden), BF16),
            pltpu.VMEM((hidden, width), BF16),
            pltpu.SemaphoreType.DMA((5,)),
            *[pltpu.SemaphoreType.DMA((chips,))] * 12,
            pltpu.SemaphoreType.DMA((2,)),
            pltpu.SemaphoreType.DMA((2,)),
        ],
        compiler_params=pltpu.CompilerParams(
            collective_id=0, has_side_effects=True, vmem_limit_bytes=56 * 1024 * 1024
        ),
    )(
        sel_blocks, hist_len, queries, keys_cache.reshape(blocked), values_cache.reshape(blocked),
        w_gate, w_up, w_down,
    )


def solution(mesh):
    placed = (
        P(("groups", "hist"), None),
        P(("groups", "hist"), None),
        P(("groups", "hist"), None),
        P("groups"),
        P("groups"),
        P(None, "hist"),
        P(None, "hist"),
        P("hist", None),
    )
    return jax.shard_map(
        functools.partial(on_device, mesh.shape["hist"]),
        mesh=mesh,
        in_specs=placed,
        out_specs=P(("groups", "hist"), None),
        check_vma=False,
    )
```

```python
import functools
import math

import jax
import jax.numpy as jnp
from jax import lax
from jax.experimental import pallas as pl
from jax.experimental.pallas import tpu as pltpu
from jax.sharding import PartitionSpec as P

HDIM = 128
BLOCK = 128
CORES = 2
COLUMN_GROUPS = 3
MESH = pl.DeviceIdType.MESH
F32 = jnp.float32
BF16 = jnp.bfloat16


def loop(start, stop, body):
    if stop - start <= 8:
        for i in range(start, stop):
            body(i)
    else:
        lax.fori_loop(start, stop, lambda i, c: (body(i), c)[1], 0)


def silu_of_twice(z):
    return z + z * jnp.tanh(z)


def pack(rows):
    half = rows.shape[1] // 2
    return jnp.concatenate([rows[:, :half], rows[:, half:]], axis=0)


def unpack(rows):
    half = rows.shape[0] // 2
    return jnp.concatenate([rows[:half], rows[half:]], axis=1)


def rms_scale(packed):
    half, width = packed.shape[0] // 2, packed.shape[1] * 2
    squares = jnp.sum(packed * packed, axis=1, keepdims=True)
    both = lax.rsqrt((squares[:half] + squares[half:]) / width + 1e-06)
    return jnp.concatenate([both, both], axis=0)


def kernel(
    chips, sel_ref, len_ref, q_ref, k_hbm, v_hbm, wg_hbm, wu_hbm, wd_hbm, out_ref,
    qbuf, nbuf, keep_a, obuf_a, rbuf_a, keep_f, obuf_f, rbuf_f,
    k_all, v_all, k_sel, v_sel, wg, wu, wd,
    local_sem, pair_send, pair_recv, q_send, q_recv, n_send, n_recv, a_send, a_recv, f_send, f_recv,
):
    tokens, width = q_ref.shape
    half = width // 2
    groups, span = keep_a.shape[0], keep_a.shape[2]
    slots = k_sel.shape[1]
    blocks_dev = k_all.shape[0]
    chunk = min(chips, 8)
    group = lax.axis_index("groups")
    me = lax.axis_index("hist")
    chip, core = me // CORES, me % CORES
    sibling = (group, chip * CORES + (1 - core))
    paired = chips & (chips - 1) == 0

    def peer(k, back=False):
        if paired:
            other = jnp.bitwise_xor(chip, k)
        else:
            other = lax.rem(chip + (chips - k if back else k), chips)
        return (group, other * CORES + core)

    def peers(body):
        loop(1, chips, lambda i: body(chips - i))

    locals_ = [
        pltpu.make_async_copy(src, dst, local_sem.at[i])
        for i, (src, dst) in enumerate(
            [(k_hbm, k_all), (v_hbm, v_all), (wg_hbm, wg.at[0]), (wu_hbm, wu.at[0]), (wd_hbm, wd.at[0])]
        )
    ]
    for copy in locals_:
        copy.start()

    barrier = pltpu.get_barrier_semaphore()
    pl.semaphore_signal(barrier, inc=1, device_id=sibling, device_id_type=MESH)
    peers(lambda k: pl.semaphore_signal(barrier, inc=1, device_id=peer(k), device_id_type=MESH))

    q_packed = pack(q_ref[...].astype(F32))
    qbuf[0] = q_packed.astype(BF16)

    first = me * blocks_dev

    def pick(i, state):
        count, chosen = state
        local = sel_ref[i] - first
        mine = jnp.logical_and(local >= 0, local < blocks_dev)
        hit = [jnp.logical_and(mine, count == s) for s in range(slots)]
        return count + mine.astype(jnp.int32), tuple(jnp.where(h, local, c) for h, c in zip(hit, chosen))

    zero = jnp.int32(0)
    count, chosen = lax.fori_loop(0, sel_ref.shape[0], pick, (zero, (zero,) * slots))
    row = lax.broadcasted_iota(jnp.int32, (BLOCK, 1), 0)
    locals_[0].wait()
    for s in range(slots):
        k_sel[0, s] = k_all[chosen[s]]
    locals_[1].wait()
    for s in range(slots):
        limit = jnp.where(count > s, len_ref[0] - (first + chosen[s]) * BLOCK, 0)
        block = v_all[chosen[s]]
        v_sel[0, s] = jnp.where(row < limit, block.astype(F32), 0.0).astype(BF16)

    pl.semaphore_wait(barrier, chips)

    def pair(i, ref):
        return pltpu.make_async_remote_copy(
            ref.at[0], ref.at[1], pair_send.at[i], pair_recv.at[i], sibling, MESH
        )

    shared = [pair(i, ref) for i, ref in enumerate((k_sel, v_sel, wg, wu, wd))]

    def gather(buf, send, recv):
        return lambda k: pltpu.make_async_remote_copy(
            buf.at[0], buf.at[k], send.at[k], recv.at[k], peer(k), MESH
        )

    def scatter(obuf, rbuf, send, recv):
        return lambda g, k: pltpu.make_async_remote_copy(
            obuf.at[k, g], rbuf.at[k, g], send.at[k, g], recv.at[k, g], peer(k, True), MESH
        )

    queries = gather(qbuf, q_send, q_recv)
    normals = gather(nbuf, n_send, n_recv)
    attended = scatter(obuf_a, rbuf_a, a_send, a_recv)
    hidden = scatter(obuf_f, rbuf_f, f_send, f_recv)

    def total(copy, keep, rbuf):
        parts = []
        for g in range(groups):
            part = keep[g]
            if chips <= 8:
                for k in range(1, chips):
                    copy(g, k).wait_recv()
                    part = part + rbuf[k, g].astype(F32)
            else:

                def add(k, part, g=g):
                    copy(g, k).wait_recv()
                    return part + rbuf[k, g].astype(F32)

                part = lax.fori_loop(1, chips, add, part)
            parts.append(part)
        return jnp.concatenate(parts, axis=1)

    def put(i, g, columns, left, right, keep, obuf):
        w = left.shape[-1]
        both = jnp.concatenate([x.reshape(chunk, tokens, w) for x in (left, right)], axis=1)
        obuf[pl.ds(i * chunk, chunk), g, :, columns] = both.astype(BF16)

        def own():
            keep[g, :, columns] = both[0]

        if isinstance(i, int):
            if i == 0:
                own()
        else:
            pl.when(i == 0)(own)

    def halves(block):
        w = block.shape[-1]
        block = block.astype(F32).reshape(chunk, 2, tokens, w)
        return [block[:, i].reshape(chunk * tokens, w).astype(BF16) for i in range(2)]

    peers(lambda k: queries(k).start())
    shared[0].start()
    shared[1].start()
    peers(lambda k: queries(k).wait_recv())
    shared[0].wait_recv()
    shared[1].wait_recv()
    for copy in locals_[2:]:
        copy.wait()
    for copy in shared[2:]:
        copy.start()

    half_scale = 0.5 / math.sqrt(HDIM)

    def head(query, columns):
        keys = k_sel[:, :, :, columns].reshape(CORES * slots * BLOCK, HDIM)
        values = v_sel[:, :, :, columns].reshape(CORES * slots * BLOCK, HDIM)
        scores = lax.dot_general(query, keys, (((1,), (1,)), ((), ())), preferred_element_type=F32)
        weights = silu_of_twice(scores * half_scale).astype(BF16)
        return jnp.dot(weights, values, preferred_element_type=F32)

    for g in range(groups):

        def attend(i, g=g):
            for j in range(span // HDIM):
                at = g * span + j * HDIM
                left, right = halves(qbuf[pl.ds(i * chunk, chunk), :, pl.ds(at, HDIM)])
                left, right = head(left, pl.ds(at, HDIM)), head(right, pl.ds(half + at, HDIM))
                put(i, g, pl.ds(j * HDIM, HDIM), left, right, keep_a, obuf_a)

        loop(0, chips // chunk, attend)
        peers(lambda k, g=g: attended(g, k).start())

    attention = total(attended, keep_a, rbuf_a)
    stream = q_packed + attention * rms_scale(attention)
    nbuf[0] = (stream * rms_scale(stream)).astype(BF16)
    peers(lambda k: normals(k).start())
    for copy in shared[2:]:
        copy.wait_recv()
    peers(lambda k: normals(k).wait_recv())

    def activate(i):
        left, right = halves(nbuf[pl.ds(i * chunk, chunk)])

        def project(w):
            top = jnp.dot(left, w[:half], preferred_element_type=F32)
            return top + jnp.dot(right, w[half:], preferred_element_type=F32)

        return [
            (silu_of_twice(0.5 * project(wg.at[c])) * project(wu.at[c])).astype(BF16) for c in range(CORES)
        ]

    def feed(i, g, activation):
        def down(columns):
            return sum(
                jnp.dot(activation[c], wd[c, :, columns], preferred_element_type=F32) for c in range(CORES)
            )

        left, right = down(pl.ds(g * span, span)), down(pl.ds(half + g * span, span))
        put(i, g, slice(None), left, right, keep_f, obuf_f)

    if chips == chunk:
        activation = activate(0)
        for g in range(groups):
            feed(0, g, activation)
            peers(lambda k, g=g: hidden(g, k).start())
    else:

        def feed_all(i):
            activation = activate(i)
            for g in range(groups):
                feed(i, g, activation)

        loop(0, chips // chunk, feed_all)
        for g in range(groups):
            peers(lambda k, g=g: hidden(g, k).start())

    out_ref[...] = unpack(stream + total(hidden, keep_f, rbuf_f)).astype(out_ref.dtype)

    for copy in shared:
        copy.wait_send()
    peers(lambda k: queries(k).wait_send())
    peers(lambda k: normals(k).wait_send())
    for g in range(groups):
        peers(lambda k, g=g: attended(g, k).wait_send())
        peers(lambda k, g=g: hidden(g, k).wait_send())


def on_device(hist, queries, keys_cache, values_cache, sel_blocks, hist_len, w_gate, w_up, w_down):
    chips = hist // CORES
    tokens, width = queries.shape
    blocks_dev = keys_cache.shape[0] // BLOCK
    slots = max(1, blocks_dev // 2)
    hidden = w_gate.shape[1]
    blocked = (blocks_dev, BLOCK, width)
    packed = (2 * tokens, width // 2)
    groups = COLUMN_GROUPS if (width // 2) % (COLUMN_GROUPS * HDIM) == 0 else 1
    pieces = (groups, 2 * tokens, width // 2 // groups)
    exchange = [
        pltpu.VMEM(pieces, F32),
        pltpu.VMEM((chips,) + pieces, BF16),
        pltpu.VMEM((chips,) + pieces, BF16),
    ]
    smem = pl.BlockSpec(memory_space=pltpu.SMEM)
    vmem = pl.BlockSpec(memory_space=pltpu.VMEM)
    anywhere = pl.BlockSpec(memory_space=pl.ANY)
    return pl.pallas_call(
        functools.partial(kernel, chips),
        out_shape=jax.ShapeDtypeStruct((tokens, width), BF16),
        in_specs=[smem, smem, vmem] + [anywhere] * 5,
        out_specs=vmem,
        scratch_shapes=[
            pltpu.VMEM((chips,) + packed, BF16),
            pltpu.VMEM((chips,) + packed, BF16),
            *exchange,
            *exchange,
            pltpu.VMEM(blocked, BF16),
            pltpu.VMEM(blocked, BF16),
            pltpu.VMEM((CORES, slots, BLOCK, width), BF16),
            pltpu.VMEM((CORES, slots, BLOCK, width), BF16),
            pltpu.VMEM((CORES, width, hidden), BF16),
            pltpu.VMEM((CORES, width, hidden), BF16),
            pltpu.VMEM((CORES, hidden, width), BF16),
            *[pltpu.SemaphoreType.DMA((5,))] * 3,
            *[pltpu.SemaphoreType.DMA((chips,))] * 4,
            *[pltpu.SemaphoreType.DMA((chips, groups))] * 4,
        ],
        compiler_params=pltpu.CompilerParams(
            collective_id=0, has_side_effects=True, vmem_limit_bytes=56 * 1024 * 1024
        ),
    )(
        sel_blocks, hist_len, queries, keys_cache.reshape(blocked), values_cache.reshape(blocked),
        w_gate, w_up, w_down,
    )


def solution(mesh):
    placed = (
        P(("groups", "hist"), None),
        P(("groups", "hist"), None),
        P(("groups", "hist"), None),
        P("groups"),
        P("groups"),
        P(None, "hist"),
        P(None, "hist"),
        P("hist", None),
    )
    return jax.shard_map(
        functools.partial(on_device, mesh.shape["hist"]),
        mesh=mesh,
        in_specs=placed,
        out_specs=P(("groups", "hist"), None),
        check_vma=False,
    )
```

```python
import functools
import math

import jax
import jax.numpy as jnp
from jax import lax
from jax.experimental import pallas as pl
from jax.experimental.pallas import tpu as pltpu
from jax.sharding import PartitionSpec as P

HDIM = 128
BLOCK = 128
CORES = 2
COLUMN_GROUPS = 2
MESH = pl.DeviceIdType.MESH
F32 = jnp.float32
BF16 = jnp.bfloat16


def loop(start, stop, body):
    if stop - start <= 8:
        for i in range(start, stop):
            body(i)
    else:
        lax.fori_loop(start, stop, lambda i, c: (body(i), c)[1], 0)


def silu_of_twice(z):
    return z + z * jnp.tanh(z)


def pack(rows):
    half = rows.shape[1] // 2
    return jnp.concatenate([rows[:, :half], rows[:, half:]], axis=0)


def unpack(rows):
    half = rows.shape[0] // 2
    return jnp.concatenate([rows[:half], rows[half:]], axis=1)


def rms_scale(packed):
    half, width = packed.shape[0] // 2, packed.shape[1] * 2
    squares = jnp.sum(packed * packed, axis=1, keepdims=True)
    both = lax.rsqrt((squares[:half] + squares[half:]) / width + 1e-06)
    return jnp.concatenate([both, both], axis=0)


def kernel(
    chips, sel_ref, len_ref, q_ref, k_hbm, v_hbm, wg_hbm, wu_hbm, wd_hbm, out_ref,
    qbuf, nbuf, keep_a, obuf_a, rbuf_a, keep_f, obuf_f, rbuf_f,
    k_all, v_all, k_sel, v_sel, wg, wu, wd,
    local_sem, pair_send, pair_recv, q_send, q_recv, n_send, n_recv, a_send, a_recv, f_send, f_recv,
):
    tokens, width = q_ref.shape
    half = width // 2
    groups, span = keep_a.shape[0], keep_a.shape[2]
    slots = k_sel.shape[1]
    blocks_dev = k_all.shape[0]
    chunk = min(chips, 8)
    group = lax.axis_index("groups")
    me = lax.axis_index("hist")
    chip, core = me // CORES, me % CORES
    sibling = (group, chip * CORES + (1 - core))
    paired = chips & (chips - 1) == 0

    def peer(k, back=False):
        if paired:
            other = jnp.bitwise_xor(chip, k)
        else:
            other = lax.rem(chip + (chips - k if back else k), chips)
        return (group, other * CORES + core)

    def peers(body):
        loop(1, chips, lambda i: body(chips - i))

    locals_ = [
        pltpu.make_async_copy(src, dst, local_sem.at[i])
        for i, (src, dst) in enumerate(
            [(k_hbm, k_all), (v_hbm, v_all), (wg_hbm, wg.at[0]), (wu_hbm, wu.at[0]), (wd_hbm, wd.at[0])]
        )
    ]
    for copy in locals_:
        copy.start()

    barrier = pltpu.get_barrier_semaphore()
    pl.semaphore_signal(barrier, inc=1, device_id=sibling, device_id_type=MESH)
    peers(lambda k: pl.semaphore_signal(barrier, inc=1, device_id=peer(k), device_id_type=MESH))

    q_packed = pack(q_ref[...].astype(F32))
    qbuf[0] = q_packed.astype(BF16)

    first = me * blocks_dev

    def pick(i, state):
        count, chosen = state
        local = sel_ref[i] - first
        mine = jnp.logical_and(local >= 0, local < blocks_dev)
        hit = [jnp.logical_and(mine, count == s) for s in range(slots)]
        return count + mine.astype(jnp.int32), tuple(jnp.where(h, local, c) for h, c in zip(hit, chosen))

    zero = jnp.int32(0)
    count, chosen = lax.fori_loop(0, sel_ref.shape[0], pick, (zero, (zero,) * slots))
    row = lax.broadcasted_iota(jnp.int32, (BLOCK, 1), 0)
    locals_[0].wait()
    for s in range(slots):
        k_sel[0, s] = k_all[chosen[s]]
    locals_[1].wait()
    for s in range(slots):
        limit = jnp.where(count > s, len_ref[0] - (first + chosen[s]) * BLOCK, 0)
        block = v_all[chosen[s]]
        v_sel[0, s] = jnp.where(row < limit, block.astype(F32), 0.0).astype(BF16)

    pl.semaphore_wait(barrier, chips)

    def pair(i, ref):
        return pltpu.make_async_remote_copy(
            ref.at[0], ref.at[1], pair_send.at[i], pair_recv.at[i], sibling, MESH
        )

    shared = [pair(i, ref) for i, ref in enumerate((k_sel, v_sel, wg, wu, wd))]

    def gather(buf, send, recv):
        return lambda k: pltpu.make_async_remote_copy(
            buf.at[0], buf.at[k], send.at[k], recv.at[k], peer(k), MESH
        )

    def scatter(obuf, rbuf, send, recv):
        return lambda g, k: pltpu.make_async_remote_copy(
            obuf.at[k, g], rbuf.at[k, g], send.at[k, g], recv.at[k, g], peer(k, True), MESH
        )

    queries = gather(qbuf, q_send, q_recv)
    normals = gather(nbuf, n_send, n_recv)
    attended = scatter(obuf_a, rbuf_a, a_send, a_recv)
    hidden = scatter(obuf_f, rbuf_f, f_send, f_recv)

    def total(copy, keep, rbuf):
        parts = []
        for g in range(groups):
            part = keep[g]
            if chips <= 8:
                for k in range(1, chips):
                    copy(g, k).wait_recv()
                    part = part + rbuf[k, g].astype(F32)
            else:

                def add(k, part, g=g):
                    copy(g, k).wait_recv()
                    return part + rbuf[k, g].astype(F32)

                part = lax.fori_loop(1, chips, add, part)
            parts.append(part)
        return jnp.concatenate(parts, axis=1)

    def put(i, g, columns, left, right, keep, obuf):
        w = left.shape[-1]
        both = jnp.concatenate([x.reshape(chunk, tokens, w) for x in (left, right)], axis=1)
        obuf[pl.ds(i * chunk, chunk), g, :, columns] = both.astype(BF16)

        def own():
            keep[g, :, columns] = both[0]

        if isinstance(i, int):
            if i == 0:
                own()
        else:
            pl.when(i == 0)(own)

    def halves(block):
        w = block.shape[-1]
        block = block.astype(F32).reshape(chunk, 2, tokens, w)
        return [block[:, i].reshape(chunk * tokens, w).astype(BF16) for i in range(2)]

    peers(lambda k: queries(k).start())
    shared[0].start()
    shared[1].start()
    peers(lambda k: queries(k).wait_recv())
    shared[0].wait_recv()
    shared[1].wait_recv()
    for copy in locals_[2:]:
        copy.wait()
    for copy in shared[2:]:
        copy.start()

    half_scale = 0.5 / math.sqrt(HDIM)

    def head(query, columns):
        keys = k_sel[:, :, :, columns].reshape(CORES * slots * BLOCK, HDIM)
        values = v_sel[:, :, :, columns].reshape(CORES * slots * BLOCK, HDIM)
        scores = lax.dot_general(query, keys, (((1,), (1,)), ((), ())), preferred_element_type=F32)
        weights = silu_of_twice(scores * half_scale).astype(BF16)
        return jnp.dot(weights, values, preferred_element_type=F32)

    for g in range(groups):

        def attend(i, g=g):
            for j in range(span // HDIM):
                at = g * span + j * HDIM
                left, right = halves(qbuf[pl.ds(i * chunk, chunk), :, pl.ds(at, HDIM)])
                left, right = head(left, pl.ds(at, HDIM)), head(right, pl.ds(half + at, HDIM))
                put(i, g, pl.ds(j * HDIM, HDIM), left, right, keep_a, obuf_a)

        loop(0, chips // chunk, attend)
        peers(lambda k, g=g: attended(g, k).start())

    attention = total(attended, keep_a, rbuf_a)
    stream = q_packed + attention * rms_scale(attention)
    nbuf[0] = (stream * rms_scale(stream)).astype(BF16)
    peers(lambda k: normals(k).start())
    for copy in shared[2:]:
        copy.wait_recv()
    peers(lambda k: normals(k).wait_recv())

    def activate(i):
        left, right = halves(nbuf[pl.ds(i * chunk, chunk)])

        def project(w):
            top = jnp.dot(left, w[:half], preferred_element_type=F32)
            return top + jnp.dot(right, w[half:], preferred_element_type=F32)

        return [
            (silu_of_twice(0.5 * project(wg.at[c])) * project(wu.at[c])).astype(BF16) for c in range(CORES)
        ]

    def feed(i, g, activation):
        def down(columns):
            return sum(
                jnp.dot(activation[c], wd[c, :, columns], preferred_element_type=F32) for c in range(CORES)
            )

        left, right = down(pl.ds(g * span, span)), down(pl.ds(half + g * span, span))
        put(i, g, slice(None), left, right, keep_f, obuf_f)

    if chips == chunk:
        activation = activate(0)
        for g in range(groups):
            feed(0, g, activation)
            peers(lambda k, g=g: hidden(g, k).start())
    else:

        def feed_all(i):
            activation = activate(i)
            for g in range(groups):
                feed(i, g, activation)

        loop(0, chips // chunk, feed_all)
        for g in range(groups):
            peers(lambda k, g=g: hidden(g, k).start())

    out_ref[...] = unpack(stream + total(hidden, keep_f, rbuf_f))

    for copy in shared:
        copy.wait_send()
    peers(lambda k: queries(k).wait_send())
    peers(lambda k: normals(k).wait_send())
    for g in range(groups):
        peers(lambda k, g=g: attended(g, k).wait_send())
        peers(lambda k, g=g: hidden(g, k).wait_send())


def on_device(hist, queries, keys_cache, values_cache, sel_blocks, hist_len, w_gate, w_up, w_down):
    chips = hist // CORES
    tokens, width = queries.shape
    blocks_dev = keys_cache.shape[0] // BLOCK
    slots = max(1, blocks_dev // 2)
    hidden = w_gate.shape[1]
    blocked = (blocks_dev, BLOCK, width)
    packed = (2 * tokens, width // 2)
    groups = COLUMN_GROUPS if (width // 2) % (COLUMN_GROUPS * HDIM) == 0 else 1
    pieces = (groups, 2 * tokens, width // 2 // groups)
    exchange = [
        pltpu.VMEM(pieces, F32),
        pltpu.VMEM((chips,) + pieces, BF16),
        pltpu.VMEM((chips,) + pieces, BF16),
    ]
    smem = pl.BlockSpec(memory_space=pltpu.SMEM)
    vmem = pl.BlockSpec(memory_space=pltpu.VMEM)
    anywhere = pl.BlockSpec(memory_space=pl.ANY)
    return pl.pallas_call(
        functools.partial(kernel, chips),
        out_shape=jax.ShapeDtypeStruct((tokens, width), F32),
        in_specs=[smem, smem, vmem] + [anywhere] * 5,
        out_specs=vmem,
        scratch_shapes=[
            pltpu.VMEM((chips,) + packed, BF16),
            pltpu.VMEM((chips,) + packed, BF16),
            *exchange,
            *exchange,
            pltpu.VMEM(blocked, BF16),
            pltpu.VMEM(blocked, BF16),
            pltpu.VMEM((CORES, slots, BLOCK, width), BF16),
            pltpu.VMEM((CORES, slots, BLOCK, width), BF16),
            pltpu.VMEM((CORES, width, hidden), BF16),
            pltpu.VMEM((CORES, width, hidden), BF16),
            pltpu.VMEM((CORES, hidden, width), BF16),
            *[pltpu.SemaphoreType.DMA((5,))] * 3,
            *[pltpu.SemaphoreType.DMA((chips,))] * 4,
            *[pltpu.SemaphoreType.DMA((chips, groups))] * 4,
        ],
        compiler_params=pltpu.CompilerParams(
            collective_id=0, has_side_effects=True, vmem_limit_bytes=56 * 1024 * 1024
        ),
    )(
        sel_blocks, hist_len, queries, keys_cache.reshape(blocked), values_cache.reshape(blocked),
        w_gate, w_up, w_down,
    ).astype(BF16)


def solution(mesh):
    placed = (
        P(("groups", "hist"), None),
        P(("groups", "hist"), None),
        P(("groups", "hist"), None),
        P("groups"),
        P("groups"),
        P(None, "hist"),
        P(None, "hist"),
        P("hist", None),
    )
    return jax.shard_map(
        functools.partial(on_device, mesh.shape["hist"]),
        mesh=mesh,
        in_specs=placed,
        out_specs=P(("groups", "hist"), None),
        check_vma=False,
    )
```
